32 devices in a mesh: slab: 16 (over z, y, core), blk: 2 (over x).
Axes of the slice: x: 2, y: 2, z: 4, core: 2. Of those that a mesh axis runs over, the one named last changes fastest.
Arguments:
- residual: bfloat16 [16, 16, 8, 40, 128], P('slab', 'blk'), may hold values from -6 to 6
- tile_values: bfloat16 [16, 2, 5, 64, 128, 128], P('slab', 'blk'), may hold values from -0.109375 to 0.109375
- row_index: int32 [16, 2, 5, 64], P('slab', 'blk'), may hold values from 0 to 15
- voxel_index: int32 [16, 2, 5, 64], P('slab', 'blk'), may hold values from 0 to 255
- slot_count: int32 [16, 2, 5], P('slab', 'blk'), may hold values from 8 to 64, as said below
- tof_shift: int32 [40], replicated, may hold values from -20 to 19, as said below
Outputs:
- gradient_image: float32 [16, 512, 8, 128], P('slab', 'blk')
The draws below stay inside these ranges and needn't reach their ends.
Inputs may be any that keep to these rules, and one draw needn't show every extreme that they name: `slot_count`: slots at or beyond a list's count are unused; some list is full in every draw. `tof_shift`: every TOF bin has its own offset: the 40 offsets are the whole numbers of the range, each once, in an order drawn from the seed.
All inputs are finite; a program needn't handle non-finite values.
Results may differ from the reference program's by a relative error of at most 0.0003.
Values may be sent and summed in bfloat16 or wider, within the bound.
A program may use at most 128 MiB of HBM per device.

```python
import jax
import jax.numpy as jnp
from jax import lax

TILE = 128
GATES = 8
TOFB = 40
SPAN = 2
VT = 256
RT = 8
MAXT = 64
SLABS = 16
BLOCKS = 2
OFFSETS = 5


def draw_slot_count(key, part):
    key = jax.random.fold_in(key, 3)
    first_key, second_key = jax.random.split(key)
    list_shape = (SLABS, BLOCKS, OFFSETS)
    counts = jax.random.randint(first_key, list_shape, MAXT // 8, MAXT + 1, dtype=jnp.int32)
    total_lists = SLABS * BLOCKS * OFFSETS
    chosen = jax.random.randint(second_key, (), 0, total_lists, dtype=jnp.int32)
    flat_counts = counts.reshape(-1)
    filled = jnp.where(jnp.arange(total_lists, dtype=jnp.int32) == chosen, MAXT, flat_counts)
    return filled.reshape(list_shape)


def draw_tof_shift(key, part):
    key = jax.random.fold_in(key, 7)
    ordered = jnp.arange(TOFB, dtype=jnp.int32) - TOFB // 2
    return jax.random.permutation(key, ordered).astype(jnp.int32)


def plant(drawn, key, least, top_value):
    place = [jax.random.randint(jax.random.fold_in(key, axis), (), 0, length) for axis, length in enumerate(drawn.shape)]
    longest = drawn.shape.index(max(drawn.shape))
    neighbour = place[:longest] + [(place[longest] + 1) % drawn.shape[longest]] + place[longest + 1:]
    return drawn.at[tuple(place)].set(least).at[tuple(neighbour)].set(top_value)


def block_levels(key, shape, cuts, low, top_value):
    def one(axis_at, parts):
        heights = jax.random.uniform(jax.random.fold_in(jax.random.fold_in(key, 6), axis_at), (parts,), jnp.float32, low / len(cuts), top_value / len(cuts))
        return jnp.repeat(jnp.exp(heights), shape[axis_at] // parts).reshape((-1,) + (1,) * (len(shape) - axis_at - 1))

    gain = one(*cuts[0])
    for cut in cuts[1:]:
        gain = gain * one(*cut)
    return gain


def bell_draw(stream_key, dims, spread, most, shards=(), kind=jnp.bfloat16):
    values = spread * jax.random.normal(stream_key, dims, jnp.float32)
    if shards:
        values = values * block_levels(stream_key, dims, shards, -0.22, 0.18)
    return jnp.clip(values, -most, most).astype(kind)


def setup_inputs(seed: int = 0) -> dict:
    key_list = jax.random.split(jax.random.key(seed), 7)
    return {
        "residual": bell_draw(key_list[0], (SLABS, RT * BLOCKS, GATES, TOFB, TILE), 1.0, 6.0, ((0, 16), (1, 2))),
        "tile_values": bell_draw(key_list[1], (SLABS, BLOCKS, OFFSETS, MAXT, TILE, TILE), (TILE * TOFB * OFFSETS * MAXT // (2 * VT)) ** -0.5, 0.109375, ((0, 16), (1, 2))),
        "row_index": plant(jax.random.randint(key_list[2], (SLABS, BLOCKS, OFFSETS, MAXT), 0, RT * BLOCKS), jax.random.fold_in(key_list[2], 1), 0, (RT * BLOCKS) - 1).astype(jnp.int32),
        "voxel_index": plant(jax.random.randint(key_list[3], (SLABS, BLOCKS, OFFSETS, MAXT), 0, VT), jax.random.fold_in(key_list[3], 1), 0, VT - 1).astype(jnp.int32),
        "slot_count": draw_slot_count(jax.random.fold_in(key_list[6], 71), 0),
        "tof_shift": draw_tof_shift(jax.random.fold_in(key_list[6], 71), 0),
    }


def contribute(sinogram, tile_set, row_list, voxel_list, live_count, tof_shift):
    picked = jnp.take(sinogram, row_list, axis=0).astype(jnp.float32)
    products = jnp.einsum("sar,srv->sav", picked, tile_set.astype(jnp.float32))
    slot_ids = jnp.arange(MAXT, dtype=jnp.int32)
    targets = voxel_list[:, None] + tof_shift[None, :]
    usable = (slot_ids < live_count)[:, None] & (targets >= 0) & (targets < VT)
    gate_ids = jnp.arange(GATES, dtype=jnp.int32)
    flat_index = jnp.where(usable[:, None, :], targets[:, None, :] * GATES + gate_ids[None, :, None], VT * GATES).astype(jnp.int32)
    partial_sum = jnp.zeros((VT * GATES, TILE), jnp.float32)
    return partial_sum.at[flat_index.reshape(-1)].add(products.reshape(-1, TILE), mode="drop")


def reference(residual, tile_values, row_index, voxel_index, slot_count, tof_shift):
    sinograms = residual.reshape(SLABS, RT * BLOCKS, GATES * TOFB, TILE)
    over_offsets = jax.vmap(contribute, in_axes=(None, 0, 0, 0, 0, None))
    over_blocks = jax.vmap(over_offsets, in_axes=(None, 0, 0, 0, 0, None))

    def one_slab(pieces):
        return over_blocks(pieces[0], pieces[1], pieces[2], pieces[3], pieces[4], tof_shift)

    terms = lax.map(one_slab, (sinograms, tile_values, row_index, voxel_index, slot_count))
    image_sum = jnp.zeros((SLABS, BLOCKS, VT * GATES, TILE), jnp.float32)
    for offset in range(OFFSETS):
        distance = offset - SPAN
        padded = jnp.pad(terms[:, :, offset], ((SPAN, SPAN), (0, 0), (0, 0), (0, 0)))
        image_sum = image_sum + padded[SPAN - distance:SPAN - distance + SLABS]
    return image_sum.reshape(SLABS, BLOCKS * VT, GATES, TILE)
```

```python
from functools import partial

import jax
import jax.numpy as jnp
from jax import lax
from jax.experimental import pallas as pl
from jax.experimental.pallas import tpu as pltpu
from jax.sharding import PartitionSpec as P

VT = 256
UNROLL = 4
CHUNKS = 4
GROUP = 64


def sort_kernel(shift_ref, res_ref, out_ref, *, gates, bins):
    size = gates * bins
    dst = lax.broadcasted_iota(jnp.int32, (size, size), 0)
    src = lax.broadcasted_iota(jnp.int32, (size, size), 1)
    pick = ((shift_ref[...] + bins // 2) == dst // gates) & (src // bins == dst % gates)
    mat = pick.astype(jnp.float32).astype(jnp.bfloat16)
    for i in range(res_ref.shape[0]):
        out_ref[i] = jnp.dot(mat, res_ref[i], preferred_element_type=jnp.float32).astype(jnp.bfloat16)


def list_kernel(
    meta, rows, voxels, sino, tiles, *rest, gates, bins, slots, quantize, has_init
):
    rest = list(rest)
    init = rest.pop(0) if has_init else None
    if quantize:
        out, scale_out, acc, buf, sems = rest
    else:
        out, acc, buf, sems = rest
    which = meta[0]
    count = meta[1]
    per = slots // CHUNKS
    half = bins // 2
    size = gates * bins

    def chunk_copy(c):
        return pltpu.make_async_copy(
            tiles.at[which, pl.ds(c * per, per)], buf.at[pl.ds(c * per, per)], sems.at[c]
        )

    for c in range(CHUNKS):
        @pl.when(c * per < count)
        def _():
            chunk_copy(c).start()

    lead = half * gates
    span = VT * gates
    acc[0:lead] = jnp.zeros((lead, acc.shape[1]), jnp.float32)
    acc[lead + span:] = jnp.zeros((acc.shape[0] - lead - span, acc.shape[1]), jnp.float32)
    if has_init:
        acc[lead:lead + span] = init[...]
    else:
        acc[lead:lead + span] = jnp.zeros((span, acc.shape[1]), jnp.float32)

    dump = VT + bins
    for c in range(CHUNKS):
        base = c * per

        @pl.when(base < count)
        def _():
            chunk_copy(c).wait()

            def group(i, carry):
                first = base + i * UNROLL
                outs = []
                for u in range(UNROLL):
                    j = first + u
                    x = sino[rows[which, j]]
                    outs.append(jnp.dot(x, buf[j], preferred_element_type=jnp.float32))
                for u in range(UNROLL):
                    j = first + u
                    v = jnp.where(j < count, voxels[which, j], dump)
                    at = pl.ds(pl.multiple_of(v * gates, gates), size)
                    acc[at] += outs[u]
                return carry

            here = jnp.minimum(count - base, per)
            lax.fori_loop(0, (here + UNROLL - 1) // UNROLL, group, 0)

    if quantize:
        groups = span // GROUP
        vals = acc[lead:lead + span].reshape(groups, GROUP, acc.shape[1])
        top = jnp.maximum(jnp.max(jnp.abs(vals), axis=1), 1e-30)
        scale_out[...] = top * (1.0 / 32767.0)
        inv = 32767.0 / top
        out[...] = jnp.round(vals * inv[:, None, :]).astype(jnp.int32).astype(jnp.int16).reshape(span, acc.shape[1])
    else:
        out[...] = acc[lead:lead + span]


def run_list(which, count, rows, voxels, sino, tiles, init, gates, bins, quantize):
    slots, depth, width = tiles.shape[1:]
    span = VT * gates
    size = gates * bins
    meta = jnp.stack([which, count]).astype(jnp.int32)
    smem = pl.BlockSpec(memory_space=pltpu.SMEM)
    vmem = pl.BlockSpec(memory_space=pltpu.VMEM)
    ins = [meta, rows, voxels, sino, tiles]
    specs = [smem, smem, smem, vmem, pl.BlockSpec(memory_space=pl.ANY)]
    if init is not None:
        ins.append(init)
        specs.append(vmem)
    if quantize:
        shape = (
            jax.ShapeDtypeStruct((span, width), jnp.int16),
            jax.ShapeDtypeStruct((span // GROUP, width), jnp.float32),
        )
        outs = (vmem, vmem)
    else:
        shape = jax.ShapeDtypeStruct((span, width), jnp.float32)
        outs = vmem
    return pl.pallas_call(
        partial(
            list_kernel, gates=gates, bins=bins, slots=slots, quantize=quantize,
            has_init=init is not None,
        ),
        out_shape=shape,
        in_specs=specs,
        out_specs=outs,
        scratch_shapes=[
            pltpu.VMEM((span + bins * gates + size, width), jnp.float32),
            pltpu.VMEM((slots, depth, width), jnp.bfloat16),
            pltpu.SemaphoreType.DMA((CHUNKS,)),
        ],
        compiler_params=pltpu.CompilerParams(vmem_limit_bytes=32 * 1024 * 1024),
        cost_estimate=pl.CostEstimate(
            flops=2 * slots * size * depth * width * 2, bytes_accessed=6_000_000, transcendentals=0
        ),
    )(*ins)


def local(residual, tile_values, row_index, voxel_index, slot_count, tof_shift):
    gates, bins, depth = residual.shape[2:]
    width = tile_values.shape[5]
    size = gates * bins
    tiles = tile_values[0, 0]
    rows = row_index[0, 0]
    voxels = voxel_index[0, 0]
    counts = slot_count[0, 0]
    shift_row = jnp.tile(tof_shift, gates).reshape(1, size)
    mine = pl.pallas_call(
        partial(sort_kernel, gates=gates, bins=bins),
        out_shape=jax.ShapeDtypeStruct((residual.shape[1], size, depth), jnp.bfloat16),
        compiler_params=pltpu.CompilerParams(vmem_limit_bytes=32 * 1024 * 1024),
    )(shift_row, residual.reshape(residual.shape[1], size, depth))
    sino = lax.all_gather(mine, "blk", axis=0, tiled=True)

    slabs = lax.axis_size("slab")
    odd = lax.rem(lax.axis_index("slab"), 2)
    sign = 2 * odd - 1
    run = partial(
        run_list, rows=rows, voxels=voxels, sino=sino, tiles=tiles, gates=gates, bins=bins
    )

    def at(distance):
        which = distance + 2
        return which, counts[which]

    mate = [(i, i ^ 1) for i in range(slabs)]

    def outward(distance):
        route = []
        for i in range(slabs):
            j = i + (distance if i % 2 else -distance)
            if 0 <= j < slabs:
                route.append((i, j))
        return route

    far_q, far_s = run(*at(2 * sign), init=None, quantize=True)
    far_q = lax.ppermute(far_q, "slab", outward(2))
    far_s = lax.ppermute(far_s, "slab", outward(2))
    in2 = run(*at(-2 * sign), init=None, quantize=False)
    in2 = lax.ppermute(in2, "slab", mate)
    in1 = run(*at(-sign), init=None, quantize=False)
    in1 = lax.ppermute(in1, "slab", mate)
    near_q, near_s = run(*at(sign), init=in2, quantize=True)
    near_q = lax.ppermute(near_q, "slab", outward(1))
    near_s = lax.ppermute(near_s, "slab", outward(1))
    own = run(*at(0 * sign), init=in1, quantize=False)

    def widen(q, s):
        q = q.astype(jnp.float32).reshape(s.shape[0], GROUP, width)
        return (q * s[:, None, :]).reshape(own.shape)

    image = own + widen(far_q, far_s) + widen(near_q, near_s)
    return image.reshape(1, VT, gates, width)


def solution(mesh):
    placed = (
        P("slab", "blk", None, None, None),
        P("slab", "blk", None, None, None, None),
        P("slab", "blk", None, None),
        P("slab", "blk", None, None),
        P("slab", "blk", None),
        P(),
    )
    return jax.shard_map(
        local, mesh=mesh, in_specs=placed, out_specs=P("slab", "blk", None, None), check_vma=False
    )
```

```python
from functools import partial

import jax
import jax.numpy as jnp
from jax import lax
from jax.experimental import pallas as pl
from jax.experimental.pallas import tpu as pltpu
from jax.sharding import PartitionSpec as P

VT = 256
UNROLL = 4
CHUNKS = 4
GROUP = 64
TOP = 32767.0
STEPS = 8.0
LIMIT = 50 * 1024 * 1024
SMEM = pl.BlockSpec(memory_space=pltpu.SMEM)
VMEM = pl.BlockSpec(memory_space=pltpu.VMEM)
HBM = pl.BlockSpec(memory_space=pl.ANY)

FAR, IN2, IN1, NEAR, OWN = range(5)


def sort_kernel(shift_ref, res_ref, out_ref, *, gates, bins):
    size = gates * bins
    dst = lax.broadcasted_iota(jnp.int32, (size, size), 0)
    src = lax.broadcasted_iota(jnp.int32, (size, size), 1)
    pick = ((shift_ref[...] + bins // 2) == dst // gates) & (src // bins == dst % gates)
    mat = pick.astype(jnp.float32).astype(jnp.bfloat16)
    for i in range(res_ref.shape[0]):
        out_ref[i] = jnp.dot(mat, res_ref[i], preferred_element_type=jnp.float32).astype(jnp.bfloat16)


def sort_rows(shift_row, res):
    count, gates, bins, depth = res.shape
    size = gates * bins
    return pl.pallas_call(
        partial(sort_kernel, gates=gates, bins=bins),
        out_shape=jax.ShapeDtypeStruct((count, size, depth), jnp.bfloat16),
        in_specs=[VMEM, VMEM],
        out_specs=VMEM,
        compiler_params=pltpu.CompilerParams(vmem_limit_bytes=LIMIT),
        cost_estimate=pl.CostEstimate(
            flops=2 * count * size * size * depth, bytes_accessed=4_000_000, transcendentals=0
        ),
    )(shift_row, res.reshape(count, size, depth))


def add_slots(acc, buf, sino, slot_of, row_of, voxel_of, total, gates, bins):
    size = gates * bins
    dump = VT + bins

    def group(i, carry):
        first = i * UNROLL
        outs = []
        ats = []
        for u in range(UNROLL):
            k = first + u
            live = k < total
            j = jnp.where(live, slot_of(k), 0)
            row = jnp.where(live, row_of(k, j), 0)
            v = jnp.where(live, voxel_of(j), dump)
            ats.append(pl.ds(pl.multiple_of(v * gates, gates), size))
            outs.append(jnp.dot(sino[row], buf[j], preferred_element_type=jnp.float32))
        for at, out in zip(ats, outs):
            acc[at] += out
        return carry

    lax.fori_loop(0, (total + UNROLL - 1) // UNROLL, group, 0)


def first_kernel(meta, rows, voxels, sino, tiles, *rest, gates, bins, slots, local_rows):
    *parts, far_slots, far_rows, far_counts, acc, buf, near_slots, sems = rest
    lists = len(parts)
    per = slots // CHUNKS
    lead = bins // 2 * gates
    span = VT * gates
    block, blocks = meta[2 * lists], meta[2 * lists + 1]

    def chunk_copy(r, c):
        return pltpu.make_async_copy(
            tiles.at[meta[r], pl.ds(c * per, per)], buf.at[r, pl.ds(c * per, per)], sems.at[r, c]
        )

    for r in range(lists):
        for c in range(CHUNKS):
            @pl.when(c * per < meta[lists + r])
            def _():
                chunk_copy(r, c).start()

    for r in range(lists):
        which, count = meta[r], meta[lists + r]

        def split(j, found):
            here, there = found
            row = rows[which, j]
            owner = row // local_rows
            mine = owner == block
            hop = block - owner
            hop = jnp.where(hop < 0, hop + blocks, hop)
            near_slots[here] = j
            far_slots[r, there] = j
            far_rows[r, there] = (hop - 1) * local_rows + row % local_rows
            step = mine.astype(jnp.int32)
            return here + step, there + 1 - step

        here, there = lax.fori_loop(0, count, split, (0, 0))
        far_counts[r] = there
        acc[...] = jnp.zeros(acc.shape, jnp.float32)
        for c in range(CHUNKS):
            @pl.when(c * per < count)
            def _():
                chunk_copy(r, c).wait()
        add_slots(
            acc, buf.at[r], sino, lambda k: near_slots[k],
            lambda k, j: rows[which, j] % local_rows, lambda j: voxels[which, j],
            here, gates, bins,
        )
        parts[r][...] = acc[lead:lead + span]


def rest_kernel(
    meta, far_slots, far_rows, far_counts, voxels, sino, tiles, init, *rest,
    role, gates, bins, slots, send, lists
):
    rest = list(rest)
    got = rest.pop(0) if role in (NEAR, OWN) else None
    out, acc, buf, sems = rest
    which, count = meta[role], meta[lists + role]
    per = slots // CHUNKS
    lead = bins // 2 * gates
    span = VT * gates

    def chunk_copy(c):
        return pltpu.make_async_copy(
            tiles.at[which, pl.ds(c * per, per)], buf.at[pl.ds(c * per, per)], sems.at[c]
        )

    for c in range(CHUNKS):
        @pl.when(c * per < count)
        def _():
            chunk_copy(c).start()

    acc[0:lead] = jnp.zeros((lead, acc.shape[1]), jnp.float32)
    acc[lead + span:] = jnp.zeros((acc.shape[0] - lead - span, acc.shape[1]), jnp.float32)
    if got is None:
        acc[lead:lead + span] = init[...]
    else:
        acc[lead:lead + span] = init[...] + got[...]
    for c in range(CHUNKS):
        @pl.when(c * per < count)
        def _():
            chunk_copy(c).wait()
    add_slots(
        acc, buf, sino, lambda k: far_slots[role, k], lambda k, j: far_rows[role, k],
        lambda j: voxels[which, j], far_counts[role], gates, bins,
    )
    if send:
        groups = span // GROUP
        vals = acc[lead:lead + span].reshape(groups, GROUP, acc.shape[1])
        top = jnp.maximum(jnp.max(jnp.abs(vals), axis=1), 1e-30)
        code = jnp.ceil(STEPS * jnp.log2(top))
        inv = TOP * jnp.exp2(code * (-1.0 / STEPS))
        q = jnp.clip(jnp.round(vals * inv[:, None, :]), -TOP, TOP)
        out[0:span] = q.astype(jnp.int32).astype(jnp.int16).reshape(span, acc.shape[1])
        out[span:] = code.astype(jnp.int32).astype(jnp.int16)
    else:
        out[...] = acc[lead:lead + span]


def local(residual, tile_values, row_index, voxel_index, slot_count, tof_shift):
    local_rows, gates, bins, depth = residual.shape[1:]
    lists, slots, _, width = tile_values.shape[2:]
    size = gates * bins
    span = VT * gates
    tiles = tile_values[0, 0]
    rows = row_index[0, 0]
    voxels = voxel_index[0, 0]
    counts = slot_count[0, 0]
    slabs = lax.axis_size("slab")
    blocks = lax.axis_size("blk")
    res = residual[0]
    others = [
        lax.ppermute(res, "blk", [(i, (i + hop) % blocks) for i in range(blocks)])
        for hop in range(1, blocks)
    ]

    sign = 2 * lax.rem(lax.axis_index("slab"), 2) - 1
    order = 2 + sign * jnp.array([2, -2, -1, 1, 0], jnp.int32)
    lived = jnp.sum(jnp.where(order[:, None] == jnp.arange(lists)[None, :], counts[None, :], 0), axis=1)
    place = jnp.stack([lax.axis_index("blk"), blocks]).astype(jnp.int32)
    meta = jnp.concatenate([order, lived.astype(jnp.int32), place])

    shift_row = jnp.tile(tof_shift, gates).reshape(1, size)
    acc = pltpu.VMEM((span + bins * gates + size, width), jnp.float32)
    image = jax.ShapeDtypeStruct((span, width), jnp.float32)
    table = jax.ShapeDtypeStruct((lists, slots), jnp.int32)
    *parts, far_slots, far_rows, far_counts = pl.pallas_call(
        partial(first_kernel, gates=gates, bins=bins, slots=slots, local_rows=local_rows),
        out_shape=[image] * lists + [table, table, jax.ShapeDtypeStruct((lists,), jnp.int32)],
        in_specs=[SMEM, SMEM, SMEM, VMEM, HBM],
        out_specs=[VMEM] * lists + [SMEM] * 3,
        scratch_shapes=[
            acc,
            pltpu.VMEM((lists, slots, depth, width), jnp.bfloat16),
            pltpu.SMEM((slots,), jnp.int32),
            pltpu.SemaphoreType.DMA((lists, CHUNKS)),
        ],
        compiler_params=pltpu.CompilerParams(vmem_limit_bytes=LIMIT),
        cost_estimate=pl.CostEstimate(
            flops=4 * lists * slots * size * depth * width, bytes_accessed=20_000_000, transcendentals=0
        ),
    )(meta, rows, voxels, sort_rows(shift_row, res), tiles)

    sino = sort_rows(shift_row, others[0] if len(others) == 1 else jnp.concatenate(others))

    def run(role, after, got=None):
        send = role in (FAR, NEAR)
        if after is not None:
            held, after = lax.optimization_barrier((meta, after))
        else:
            held = meta
        extra = [] if got is None else [got]
        shape = jax.ShapeDtypeStruct((span + span // GROUP, width), jnp.int16) if send else image
        out = pl.pallas_call(
            partial(
                rest_kernel, role=role, gates=gates, bins=bins, slots=slots, send=send, lists=lists
            ),
            out_shape=shape,
            in_specs=[SMEM] * 5 + [VMEM, HBM, VMEM] + [VMEM] * len(extra),
            out_specs=VMEM,
            scratch_shapes=[
                acc,
                pltpu.VMEM((slots, depth, width), jnp.bfloat16),
                pltpu.SemaphoreType.DMA((CHUNKS,)),
            ],
            compiler_params=pltpu.CompilerParams(vmem_limit_bytes=LIMIT),
            cost_estimate=pl.CostEstimate(
                flops=2 * slots * size * depth * width, bytes_accessed=6_000_000, transcendentals=0
            ),
        )(held, far_slots, far_rows, far_counts, voxels, sino, tiles, parts[role], *extra)
        return out, after

    mate = [(i, i ^ 1) for i in range(slabs)]

    def outward(distance):
        route = []
        for i in range(slabs):
            j = i + (distance if i % 2 else -distance)
            if 0 <= j < slabs:
                route.append((i, j))
        return route

    far, _ = run(FAR, None)
    in2, far = run(IN2, far)
    far = lax.ppermute(far, "slab", outward(2))
    in1, in2 = run(IN1, in2)
    in2 = lax.ppermute(in2, "slab", mate)
    near, in1 = run(NEAR, in1, in2)
    in1 = lax.ppermute(in1, "slab", mate)
    own, near = run(OWN, near, in1)
    near = lax.ppermute(near, "slab", outward(1))

    def widen(sent):
        scale = jnp.exp2(sent[span:].astype(jnp.float32) * (1.0 / STEPS)) * (1.0 / TOP)
        values = sent[:span].astype(jnp.float32).reshape(span // GROUP, GROUP, width)
        return (values * scale[:, None, :]).reshape(span, width)

    image_sum = own + widen(far) + widen(near)
    return image_sum.reshape(1, VT, gates, width)


def solution(mesh):
    placed = (
        P("slab", "blk", None, None, None),
        P("slab", "blk", None, None, None, None),
        P("slab", "blk", None, None),
        P("slab", "blk", None, None),
        P("slab", "blk", None),
        P(),
    )
    return jax.shard_map(
        local, mesh=mesh, in_specs=placed, out_specs=P("slab", "blk", None, None), check_vma=False
    )
```

```python
from functools import partial

import jax
import jax.numpy as jnp
from jax import lax
from jax.experimental import pallas as pl
from jax.experimental.pallas import tpu as pltpu
from jax.sharding import PartitionSpec as P

VT = 256
UNROLL = 4
CHUNKS = 4
GROUP = 64
TOP = 32767.0
STEPS = 8.0
LIMIT = 50 * 1024 * 1024
SMEM = pl.BlockSpec(memory_space=pltpu.SMEM)
VMEM = pl.BlockSpec(memory_space=pltpu.VMEM)
HBM = pl.BlockSpec(memory_space=pl.ANY)

FAR, IN2, NEAR, IN1, OWN = range(5)
REACH = (2, -2, 1, -1, 0)
SPLIT = 4
COST = pl.CostEstimate(flops=1000, bytes_accessed=1000, transcendentals=0)


def add_slots(acc, buf, sino, slot_of, row_of, voxel_of, begin, total, gates, bins):
    size = gates * bins
    dump = VT + bins

    def group(i, carry):
        first = begin + i * UNROLL
        outs = []
        ats = []
        for u in range(UNROLL):
            k = first + u
            live = k < total
            j = jnp.where(live, slot_of(k), 0)
            row = jnp.where(live, row_of(k, j), 0)
            v = jnp.where(live, voxel_of(j), dump)
            ats.append(pl.ds(pl.multiple_of(v * gates, gates), size))
            outs.append(jnp.dot(sino[row], buf[j], preferred_element_type=jnp.float32))
        for at, out in zip(ats, outs):
            acc[at] += out
        return carry

    lax.fori_loop(0, (total - begin + UNROLL - 1) // UNROLL, group, 0)


def list_of(role):
    sign = 2 * lax.rem(lax.axis_index("slab"), 2) - 1
    return REACH[0] + REACH[role] * sign


def place_of(row, local_rows):
    block, blocks = lax.axis_index("blk"), lax.axis_size("blk")
    hop = block - lax.div(row, local_rows)
    hop = jnp.where(hop < 0, hop + blocks, hop)
    return hop * local_rows + lax.rem(row, local_rows)


def sorter(shift, gates, bins):
    size = gates * bins
    src = lax.broadcasted_iota(jnp.int32, (1, size), 1)
    bin_of = lax.rem(src, bins)
    place = jnp.zeros((1, size), jnp.int32)
    for t in range(bins):
        place = jnp.where(bin_of == t, shift[t] + bins // 2, place)
    target = place * gates + lax.div(src, bins)
    dst = lax.broadcasted_iota(jnp.int32, (size, size), 0)
    return (target == dst).astype(jnp.float32).astype(jnp.bfloat16)


def reorder(mat, tile):
    return jnp.dot(mat, tile, preferred_element_type=jnp.float32).astype(jnp.bfloat16)


def join_kernel(shift, mine, others, out, *, gates, bins):
    mat = sorter(shift, gates, bins)
    local_rows = mine.shape[0]
    out[0:local_rows] = mine[...]

    def one(i, carry):
        out[local_rows + i] = reorder(mat, others[i])
        return carry

    lax.fori_loop(0, others.shape[0], one, 0, unroll=4)


def first_kernel(
    shift, counts, rows, voxels, res, tiles, *rest, gates, bins, slots
):
    *parts, sino, far_slots, far_rows, far_counts, raw, acc, buf, near_slots, raw_sem, sems = rest
    local_rows = res.shape[0]
    per = slots // CHUNKS
    lead = bins // 2 * gates
    span = VT * gates

    load = pltpu.make_async_copy(res, raw, raw_sem)
    load.start()

    def chunk_copy(r, c):
        return pltpu.make_async_copy(
            tiles.at[list_of(r), pl.ds(c * per, per)], buf.at[r, pl.ds(c * per, per)], sems.at[r, c]
        )

    for r in range(SPLIT):
        for c in range(CHUNKS):
            @pl.when(c * per < counts[list_of(r)])
            def _():
                chunk_copy(r, c).start()

    mat = sorter(shift, gates, bins)
    load.wait()
    for i in range(local_rows):
        sino[i] = reorder(mat, raw[i])

    for r in range(SPLIT):
        which = list_of(r)
        count = counts[which]

        def split(j, found):
            here, there = found
            row = place_of(rows[which, j], local_rows)
            near_slots[here] = j
            far_slots[r, there] = j
            far_rows[r, there] = row
            step = (row < local_rows).astype(jnp.int32)
            return here + step, there + 1 - step

        here, there = lax.fori_loop(0, count, split, (0, 0))
        far_counts[r] = there
        acc[...] = jnp.zeros(acc.shape, jnp.float32)
        for c in range(CHUNKS):
            @pl.when(c * per < count)
            def _():
                chunk_copy(r, c).wait()
        add_slots(
            acc, buf.at[r], sino, lambda k: near_slots[k],
            lambda k, j: lax.rem(rows[which, j], local_rows), lambda j: voxels[which, j],
            0, here, gates, bins,
        )
        parts[r][...] = acc[lead:lead + span]


def rest_kernel(
    counts, rows, voxels, far_slots, far_rows, far_counts, sino, tiles, *rest,
    role, gates, bins, slots, send, starts, local_rows
):
    starts_in, (out, acc, buf, sems) = rest[:starts], rest[starts:]
    which = list_of(role)
    count = counts[which]
    per = slots // CHUNKS
    lead = bins // 2 * gates
    span = VT * gates

    def chunk_copy(c):
        return pltpu.make_async_copy(
            tiles.at[which, pl.ds(c * per, per)], buf.at[pl.ds(c * per, per)], sems.at[c]
        )

    for c in range(CHUNKS):
        @pl.when(c * per < count)
        def _():
            chunk_copy(c).start()

    acc[0:lead] = jnp.zeros((lead, acc.shape[1]), jnp.float32)
    acc[lead + span:] = jnp.zeros((acc.shape[0] - lead - span, acc.shape[1]), jnp.float32)
    if starts == 0:
        acc[lead:lead + span] = jnp.zeros((span, acc.shape[1]), jnp.float32)
    elif starts == 1:
        acc[lead:lead + span] = starts_in[0][...]
    else:
        acc[lead:lead + span] = starts_in[0][...] + starts_in[1][...]
    for c in range(CHUNKS):
        @pl.when(c * per < count)
        def _():
            chunk_copy(c).wait()
            if role >= SPLIT:
                add_slots(
                    acc, buf, sino, lambda k: k, lambda k, j: place_of(rows[which, j], local_rows),
                    lambda j: voxels[which, j], c * per, jnp.minimum(count, (c + 1) * per), gates, bins,
                )
    if role < SPLIT:
        add_slots(
            acc, buf, sino, lambda k: far_slots[role, k], lambda k, j: far_rows[role, k],
            lambda j: voxels[which, j], 0, far_counts[role], gates, bins,
        )
    if send:
        groups = span // GROUP
        vals = acc[lead:lead + span].reshape(groups, GROUP, acc.shape[1])
        top = jnp.maximum(jnp.max(jnp.abs(vals), axis=1), 1e-30)
        code = jnp.ceil(STEPS * jnp.log2(top))
        inv = TOP * jnp.exp2(code * (-1.0 / STEPS))
        q = jnp.clip(jnp.round(vals * inv[:, None, :]), -TOP, TOP)
        out[0:span] = q.astype(jnp.int32).astype(jnp.int16).reshape(span, acc.shape[1])
        out[span:] = code.astype(jnp.int32).astype(jnp.int16)
    else:
        out[...] = acc[lead:lead + span]


def join_image(own, far, near, out):
    span, width = own.shape
    groups = span // GROUP

    def widen(sent):
        code = sent[span:].astype(jnp.int32).astype(jnp.float32)
        scale = jnp.exp2(code * (1.0 / STEPS)) * (1.0 / TOP)
        values = sent[0:span].astype(jnp.int32).astype(jnp.float32).reshape(groups, GROUP, width)
        return (values * scale[:, None, :]).reshape(span, width)

    out[...] = own[...] + widen(far) + widen(near)


def local(residual, tile_values, row_index, voxel_index, slot_count, tof_shift):
    local_rows, gates, bins, depth = residual.shape[1:]
    lists, slots, _, width = tile_values.shape[2:]
    size = gates * bins
    span = VT * gates
    tiles = tile_values[0, 0]
    rows = row_index[0, 0]
    voxels = voxel_index[0, 0]
    counts = slot_count[0, 0]
    slabs = lax.axis_size("slab")
    blocks = lax.axis_size("blk")
    res = residual[0].reshape(local_rows, size, depth)
    others = [
        lax.ppermute(res, "blk", [(i, (i + hop) % blocks) for i in range(blocks)])
        for hop in range(1, blocks)
    ]
    params = pltpu.CompilerParams(vmem_limit_bytes=LIMIT)

    acc = pltpu.VMEM((span + bins * gates + size, width), jnp.float32)
    image = jax.ShapeDtypeStruct((span, width), jnp.float32)
    table = jax.ShapeDtypeStruct((SPLIT, slots), jnp.int32)
    *parts, mine, far_slots, far_rows, far_counts = pl.pallas_call(
        partial(first_kernel, gates=gates, bins=bins, slots=slots),
        out_shape=[image] * SPLIT
        + [jax.ShapeDtypeStruct(res.shape, res.dtype)]
        + [table, table, jax.ShapeDtypeStruct((SPLIT,), jnp.int32)],
        in_specs=[SMEM] * 4 + [HBM, HBM],
        out_specs=[VMEM] * (SPLIT + 1) + [SMEM] * 3,
        scratch_shapes=[
            pltpu.VMEM(res.shape, res.dtype),
            acc,
            pltpu.VMEM((SPLIT, slots, depth, width), jnp.bfloat16),
            pltpu.SMEM((slots,), jnp.int32),
            pltpu.SemaphoreType.DMA(()),
            pltpu.SemaphoreType.DMA((SPLIT, CHUNKS)),
        ],
        compiler_params=params,
        cost_estimate=COST,
    )(tof_shift, counts, rows, voxels, res, tiles)

    sino = pl.pallas_call(
        partial(join_kernel, gates=gates, bins=bins),
        out_shape=jax.ShapeDtypeStruct((local_rows * blocks, size, depth), jnp.bfloat16),
        in_specs=[SMEM, VMEM, VMEM],
        out_specs=VMEM,
        compiler_params=params,
        cost_estimate=COST,
    )(tof_shift, mine, others[0] if len(others) == 1 else jnp.concatenate(others))

    def run(role, after, got=None):
        send = role in (FAR, NEAR)
        held = counts
        if after is not None:
            held, after = lax.optimization_barrier((counts, after))
        starts = [parts[role]] if role < SPLIT else []
        starts += [] if got is None else [got]
        out = pl.pallas_call(
            partial(
                rest_kernel, role=role, gates=gates, bins=bins, slots=slots, send=send,
                starts=len(starts), local_rows=local_rows,
            ),
            out_shape=(
                jax.ShapeDtypeStruct((span + span // GROUP, width), jnp.int16) if send else image
            ),
            in_specs=[SMEM] * 6 + [VMEM, HBM] + [VMEM] * len(starts),
            out_specs=VMEM,
            scratch_shapes=[
                acc,
                pltpu.VMEM((slots, depth, width), jnp.bfloat16),
                pltpu.SemaphoreType.DMA((CHUNKS,)),
            ],
            compiler_params=params,
            cost_estimate=COST,
        )(held, rows, voxels, far_slots, far_rows, far_counts, sino, tiles, *starts)
        return out, after

    mate = [(i, i ^ 1) for i in range(slabs)]

    def outward(distance):
        route = []
        for i in range(slabs):
            j = i + (distance if i % 2 else -distance)
            if 0 <= j < slabs:
                route.append((i, j))
        return route

    in2, _ = run(IN2, None)
    in1, in2 = run(IN1, in2)
    in2 = lax.ppermute(in2, "slab", mate)
    far, in1 = run(FAR, in1)
    in1 = lax.ppermute(in1, "slab", mate)
    near, far = run(NEAR, far, in2)
    far = lax.ppermute(far, "slab", outward(2))
    own, near = run(OWN, near, in1)
    near = lax.ppermute(near, "slab", outward(1))
    image_sum = pl.pallas_call(
        join_image,
        out_shape=image,
        in_specs=[VMEM] * 3,
        out_specs=VMEM,
        compiler_params=params,
        cost_estimate=COST,
    )(own, far, near)
    return image_sum.reshape(1, VT, gates, width)


def solution(mesh):
    placed = (
        P("slab", "blk", None, None, None),
        P("slab", "blk", None, None, None, None),
        P("slab", "blk", None, None),
        P("slab", "blk", None, None),
        P("slab", "blk", None),
        P(),
    )
    return jax.shard_map(
        local, mesh=mesh, in_specs=placed, out_specs=P("slab", "blk", None, None), check_vma=False
    )
```

```python
from functools import partial

import jax
import jax.numpy as jnp
from jax import lax
from jax.experimental import pallas as pl
from jax.experimental.pallas import tpu as pltpu
from jax.sharding import PartitionSpec as P

VT = 256
UNROLL = 4
CHUNKS = 4
GROUP = 64
TOP = 32767.0
STEPS = 8.0
LIMIT = 50 * 1024 * 1024
SMEM = pl.BlockSpec(memory_space=pltpu.SMEM)
VMEM = pl.BlockSpec(memory_space=pltpu.VMEM)
HBM = pl.BlockSpec(memory_space=pl.ANY)

FAR, IN2, NEAR, IN1, OWN = range(5)
REACH = (2, -2, 1, -1, 0)
PIECES = 2
SPLIT = 3
COST = pl.CostEstimate(flops=1000, bytes_accessed=1000, transcendentals=0)


def add_slots(acc, buf, sino, slot_of, row_of, voxel_of, begin, total, gates, bins):
    size = gates * bins
    dump = VT + bins

    def group(i, carry):
        first = begin + i * UNROLL
        outs = []
        ats = []
        for u in range(UNROLL):
            k = first + u
            live = k < total
            j = jnp.where(live, slot_of(k), 0)
            row = jnp.where(live, row_of(k, j), 0)
            v = jnp.where(live, voxel_of(j), dump)
            ats.append(pl.ds(pl.multiple_of(v * gates, gates), size))
            outs.append(jnp.dot(sino[row], buf[j], preferred_element_type=jnp.float32))
        for at, out in zip(ats, outs):
            acc[at] += out
        return carry

    lax.fori_loop(0, (total - begin + UNROLL - 1) // UNROLL, group, 0)


def list_of(role):
    sign = 2 * lax.rem(lax.axis_index("slab"), 2) - 1
    return REACH[0] + REACH[role] * sign


def place_of(row, local_rows):
    block, blocks = lax.axis_index("blk"), lax.axis_size("blk")
    hop = block - lax.div(row, local_rows)
    hop = jnp.where(hop < 0, hop + blocks, hop)
    return hop * local_rows + lax.rem(row, local_rows)


def sorter(shift, gates, bins):
    size = gates * bins
    src = lax.broadcasted_iota(jnp.int32, (1, size), 1)
    bin_of = lax.rem(src, bins)
    place = jnp.zeros((1, size), jnp.int32)
    for t in range(bins):
        place = jnp.where(bin_of == t, shift[t] + bins // 2, place)
    target = place * gates + lax.div(src, bins)
    dst = lax.broadcasted_iota(jnp.int32, (size, size), 0)
    return (target == dst).astype(jnp.float32).astype(jnp.bfloat16)


def reorder(mat, tile):
    return jnp.dot(mat, tile, preferred_element_type=jnp.float32).astype(jnp.bfloat16)


def join_kernel(shift, mine, others, out, *, gates, bins):
    mat = sorter(shift, gates, bins)
    local_rows = mine.shape[0]
    out[0:local_rows] = mine[...]

    def one(i, carry):
        out[local_rows + i] = reorder(mat, others[i])
        return carry

    lax.fori_loop(0, others.shape[0], one, 0, unroll=4)


def first_kernel(
    shift, counts, rows, voxels, res, tiles, *rest, gates, bins, slots
):
    *parts, sino, far_slots, far_rows, far_counts, raw, acc, buf, near_slots, raw_sem, sems = rest
    local_rows = res.shape[0]
    per = slots // CHUNKS
    lead = bins // 2 * gates
    span = VT * gates

    load = pltpu.make_async_copy(res, raw, raw_sem)
    load.start()

    def chunk_copy(r, c):
        return pltpu.make_async_copy(
            tiles.at[list_of(r), pl.ds(c * per, per)], buf.at[r, pl.ds(c * per, per)], sems.at[r, c]
        )

    for r in range(SPLIT):
        for c in range(CHUNKS):
            @pl.when(c * per < counts[list_of(r)])
            def _():
                chunk_copy(r, c).start()

    mat = sorter(shift, gates, bins)
    load.wait()
    for i in range(local_rows):
        sino[i] = reorder(mat, raw[i])

    for r in range(SPLIT):
        which = list_of(r)
        count = counts[which]

        def split(j, found):
            here, there = found
            row = place_of(rows[which, j], local_rows)
            near_slots[here] = j
            far_slots[r, there] = j
            far_rows[r, there] = row
            step = (row < local_rows).astype(jnp.int32)
            return here + step, there + 1 - step

        here, there = lax.fori_loop(0, count, split, (0, 0))
        far_counts[r] = there
        acc[...] = jnp.zeros(acc.shape, jnp.float32)
        for c in range(CHUNKS):
            @pl.when(c * per < count)
            def _():
                chunk_copy(r, c).wait()
        add_slots(
            acc, buf.at[r], sino, lambda k: near_slots[k],
            lambda k, j: lax.rem(rows[which, j], local_rows), lambda j: voxels[which, j],
            0, here, gates, bins,
        )
        parts[r][...] = acc[lead:lead + span]


def rest_kernel(
    counts, rows, voxels, far_slots, far_rows, far_counts, sino, tiles, *rest,
    role, gates, bins, slots, send, starts, gots, local_rows
):
    first, got, (*out, acc, buf, sems) = rest[:starts], rest[starts:starts + gots], rest[starts + gots:]
    which = list_of(role)
    count = counts[which]
    per = slots // CHUNKS
    lead = bins // 2 * gates
    span = VT * gates

    def chunk_copy(c):
        return pltpu.make_async_copy(
            tiles.at[which, pl.ds(c * per, per)], buf.at[pl.ds(c * per, per)], sems.at[c]
        )

    for c in range(CHUNKS):
        @pl.when(c * per < count)
        def _():
            chunk_copy(c).start()

    acc[0:lead] = jnp.zeros((lead, acc.shape[1]), jnp.float32)
    acc[lead + span:] = jnp.zeros((acc.shape[0] - lead - span, acc.shape[1]), jnp.float32)
    if starts:
        acc[lead:lead + span] = first[0][...]
    else:
        acc[lead:lead + span] = jnp.zeros((span, acc.shape[1]), jnp.float32)
    for i, piece in enumerate(got):
        size = span // gots
        acc[lead + i * size:lead + (i + 1) * size] += widen(piece)
    for c in range(CHUNKS):
        @pl.when(c * per < count)
        def _():
            chunk_copy(c).wait()
            if role >= SPLIT:
                add_slots(
                    acc, buf, sino, lambda k: k, lambda k, j: place_of(rows[which, j], local_rows),
                    lambda j: voxels[which, j], c * per, jnp.minimum(count, (c + 1) * per), gates, bins,
                )
    if role < SPLIT:
        add_slots(
            acc, buf, sino, lambda k: far_slots[role, k], lambda k, j: far_rows[role, k],
            lambda j: voxels[which, j], 0, far_counts[role], gates, bins,
        )
    if not send:
        out[0][...] = acc[lead:lead + span]
    else:
        for i, piece in enumerate(out):
            size = span // len(out)
            encode(acc[lead + i * size:lead + (i + 1) * size], piece)


def encode(image, out):
    span, width = image.shape
    values = image.reshape(span // GROUP, GROUP, width)
    top = jnp.maximum(jnp.max(jnp.abs(values), axis=1), 1e-30)
    code = jnp.ceil(STEPS * jnp.log2(top))
    inv = TOP * jnp.exp2(code * (-1.0 / STEPS))
    q = jnp.clip(jnp.round(values * inv[:, None, :]), -TOP, TOP)
    out[0:span] = q.astype(jnp.int32).astype(jnp.int16).reshape(span, width)
    out[span:] = code.astype(jnp.int32).astype(jnp.int16)


def widen(sent):
    span, width = sent.shape[0] * GROUP // (GROUP + 1), sent.shape[1]
    code = sent[span:].astype(jnp.int32).astype(jnp.float32)
    scale = jnp.exp2(code * (1.0 / STEPS)) * (1.0 / TOP)
    values = sent[0:span].astype(jnp.int32).astype(jnp.float32)
    values = values.reshape(span // GROUP, GROUP, width) * scale[:, None, :]
    return values.reshape(span, width)


def join_image(own, far, near, *rest):
    *pair, out = rest
    size = own.shape[0] // len(pair)
    out[...] = own[...] + widen(far) + widen(near)
    for i, piece in enumerate(pair):
        out[i * size:(i + 1) * size] += widen(piece)


def local(residual, tile_values, row_index, voxel_index, slot_count, tof_shift):
    local_rows, gates, bins, depth = residual.shape[1:]
    lists, slots, _, width = tile_values.shape[2:]
    size = gates * bins
    span = VT * gates
    tiles = tile_values[0, 0]
    rows = row_index[0, 0]
    voxels = voxel_index[0, 0]
    counts = slot_count[0, 0]
    slabs = lax.axis_size("slab")
    blocks = lax.axis_size("blk")
    res = residual[0].reshape(local_rows, size, depth)
    others = [
        lax.ppermute(res, "blk", [(i, (i + hop) % blocks) for i in range(blocks)])
        for hop in range(1, blocks)
    ]
    params = pltpu.CompilerParams(vmem_limit_bytes=LIMIT)

    acc = pltpu.VMEM((span + bins * gates + size, width), jnp.float32)
    image = jax.ShapeDtypeStruct((span, width), jnp.float32)
    table = jax.ShapeDtypeStruct((SPLIT, slots), jnp.int32)
    *parts, mine, far_slots, far_rows, far_counts = pl.pallas_call(
        partial(first_kernel, gates=gates, bins=bins, slots=slots),
        out_shape=[image] * SPLIT
        + [jax.ShapeDtypeStruct(res.shape, res.dtype)]
        + [table, table, jax.ShapeDtypeStruct((SPLIT,), jnp.int32)],
        in_specs=[SMEM] * 4 + [HBM, HBM],
        out_specs=[VMEM] * (SPLIT + 1) + [SMEM] * 3,
        scratch_shapes=[
            pltpu.VMEM(res.shape, res.dtype),
            acc,
            pltpu.VMEM((SPLIT, slots, depth, width), jnp.bfloat16),
            pltpu.SMEM((slots,), jnp.int32),
            pltpu.SemaphoreType.DMA(()),
            pltpu.SemaphoreType.DMA((SPLIT, CHUNKS)),
        ],
        compiler_params=params,
        cost_estimate=COST,
    )(tof_shift, counts, rows, voxels, res, tiles)

    sino = pl.pallas_call(
        partial(join_kernel, gates=gates, bins=bins),
        out_shape=jax.ShapeDtypeStruct((local_rows * blocks, size, depth), jnp.bfloat16),
        in_specs=[SMEM, VMEM, VMEM],
        out_specs=VMEM,
        compiler_params=params,
        cost_estimate=COST,
    )(tof_shift, mine, others[0] if len(others) == 1 else jnp.concatenate(others))

    def run(role, after, got=()):
        held = counts
        if after is not None:
            held, after = lax.optimization_barrier((counts, after))
        starts = [parts[role]] if role < SPLIT else []
        pieces = {OWN: 0, IN1: PIECES, IN2: PIECES}.get(role, 1)
        rows_out = span // max(pieces, 1)
        shape = jax.ShapeDtypeStruct((rows_out + rows_out // GROUP, width), jnp.int16)
        out = pl.pallas_call(
            partial(
                rest_kernel, role=role, gates=gates, bins=bins, slots=slots, send=pieces > 0,
                starts=len(starts), gots=len(got), local_rows=local_rows,
            ),
            out_shape=[shape] * pieces if pieces else [image],
            in_specs=[SMEM] * 6 + [VMEM, HBM] + [VMEM] * (len(starts) + len(got)),
            out_specs=[VMEM] * max(pieces, 1),
            scratch_shapes=[
                acc,
                pltpu.VMEM((slots, depth, width), jnp.bfloat16),
                pltpu.SemaphoreType.DMA((CHUNKS,)),
            ],
            compiler_params=params,
            cost_estimate=COST,
        )(held, rows, voxels, far_slots, far_rows, far_counts, sino, tiles, *starts, *got)
        return out, after

    def pass_on(sent, route):
        return [lax.ppermute(piece, "slab", route) for piece in sent]

    mate = [(i, i ^ 1) for i in range(slabs)]

    def outward(distance):
        route = []
        for i in range(slabs):
            j = i + (distance if i % 2 else -distance)
            if 0 <= j < slabs:
                route.append((i, j))
        return route

    in2, _ = run(IN2, None)
    far, in2 = run(FAR, in2)
    near, far = run(NEAR, far, pass_on(in2, mate))
    far = pass_on(far, outward(2))
    in1, near = run(IN1, near)
    near = pass_on(near, outward(1))
    own, in1 = run(OWN, in1)
    in1 = pass_on(in1, mate)
    image_sum = pl.pallas_call(
        join_image,
        out_shape=image,
        in_specs=[VMEM] * (3 + PIECES),
        out_specs=VMEM,
        compiler_params=params,
        cost_estimate=COST,
    )(*own, *far, *near, *in1)
    return image_sum.reshape(1, VT, gates, width)


def solution(mesh):
    placed = (
        P("slab", "blk", None, None, None),
        P("slab", "blk", None, None, None, None),
        P("slab", "blk", None, None),
        P("slab", "blk", None, None),
        P("slab", "blk", None),
        P(),
    )
    return jax.shard_map(
        local, mesh=mesh, in_specs=placed, out_specs=P("slab", "blk", None, None), check_vma=False
    )
```

```python
from functools import partial

import jax
import jax.numpy as jnp
from jax import lax
from jax.experimental import pallas as pl
from jax.experimental.pallas import tpu as pltpu
from jax.sharding import PartitionSpec as P

VT = 256
UNROLL = 4
CHUNKS = 4
GROUP = 64
TOP = 32767.0
STEPS = 8.0
LIMIT = 43 * 1024 * 1024
SMEM = pl.BlockSpec(memory_space=pltpu.SMEM)
VMEM = pl.BlockSpec(memory_space=pltpu.VMEM)
HBM = pl.BlockSpec(memory_space=pltpu.HBM)

FAR, IN2, NEAR, IN1, OWN = range(5)
REACH = (2, -2, 1, -1, 0)
PIECES = 2
SPLIT = 3
COST = pl.CostEstimate(flops=1000, bytes_accessed=1000, transcendentals=0)


def add_slots(acc, buf, sino, slot_of, row_of, voxel_of, begin, total, gates, bins):
    size = gates * bins
    dump = VT + bins

    def group(i, carry):
        first = begin + i * UNROLL
        outs = []
        ats = []
        for u in range(UNROLL):
            k = first + u
            live = k < total
            j = jnp.where(live, slot_of(k), 0)
            row = jnp.where(live, row_of(k, j), 0)
            v = jnp.where(live, voxel_of(j), dump)
            ats.append(pl.ds(pl.multiple_of(v * gates, gates), size))
            outs.append(jnp.dot(sino[row], buf[j], preferred_element_type=jnp.float32))
        for at, out in zip(ats, outs):
            acc[at] += out
        return carry

    lax.fori_loop(0, (total - begin + UNROLL - 1) // UNROLL, group, 0)


def list_of(role):
    sign = 2 * lax.rem(lax.axis_index("slab"), 2) - 1
    return REACH[0] + REACH[role] * sign


def place_of(row, local_rows):
    block, blocks = lax.axis_index("blk"), lax.axis_size("blk")
    hop = block - lax.div(row, local_rows)
    hop = jnp.where(hop < 0, hop + blocks, hop)
    return hop * local_rows + lax.rem(row, local_rows)


def sorter(shift, gates, bins):
    size = gates * bins
    src = lax.broadcasted_iota(jnp.int32, (1, size), 1)
    bin_of = lax.rem(src, bins)
    place = jnp.zeros((1, size), jnp.int32)
    for t in range(bins):
        place = jnp.where(bin_of == t, shift[t] + bins // 2, place)
    target = place * gates + lax.div(src, bins)
    dst = lax.broadcasted_iota(jnp.int32, (size, size), 0)
    return (target == dst).astype(jnp.float32).astype(jnp.bfloat16)


def reorder(mat, tile):
    return jnp.dot(mat, tile, preferred_element_type=jnp.float32).astype(jnp.bfloat16)


def join_kernel(shift, mine, others, out, *, gates, bins):
    mat = sorter(shift, gates, bins)
    local_rows = mine.shape[0]
    out[0:local_rows] = mine[...]

    def one(i, carry):
        out[local_rows + i] = reorder(mat, others[i])
        return carry

    lax.fori_loop(0, others.shape[0], one, 0, unroll=4)


def first_kernel(
    shift, counts, rows, voxels, res, tiles, *rest, gates, bins, slots
):
    *parts, sino, buf, far_slots, far_rows, far_counts, raw, acc, near_slots, raw_sem, sems = rest
    local_rows = res.shape[0]
    per = slots // CHUNKS
    lead = bins // 2 * gates
    span = VT * gates

    load = pltpu.make_async_copy(res, raw, raw_sem)
    load.start()

    def chunk_copy(r, c):
        return pltpu.make_async_copy(
            tiles.at[list_of(r), pl.ds(c * per, per)], buf.at[r, pl.ds(c * per, per)], sems.at[r, c]
        )

    for r in range(SPLIT):
        for c in range(CHUNKS):
            @pl.when(c * per < counts[list_of(r)])
            def _():
                chunk_copy(r, c).start()

    mat = sorter(shift, gates, bins)
    load.wait()
    for i in range(local_rows):
        sino[i] = reorder(mat, raw[i])

    for r in range(SPLIT):
        which = list_of(r)
        count = counts[which]

        def split(j, found):
            here, there = found
            row = place_of(rows[which, j], local_rows)
            near_slots[here] = j
            far_slots[r, there] = j
            far_rows[r, there] = row
            step = (row < local_rows).astype(jnp.int32)
            return here + step, there + 1 - step

        here, there = lax.fori_loop(0, count, split, (0, 0))
        far_counts[r] = there
        acc[...] = jnp.zeros(acc.shape, jnp.float32)
        for c in range(CHUNKS):
            @pl.when(c * per < count)
            def _():
                chunk_copy(r, c).wait()
        add_slots(
            acc, buf.at[r], sino, lambda k: near_slots[k],
            lambda k, j: lax.rem(rows[which, j], local_rows), lambda j: voxels[which, j],
            0, here, gates, bins,
        )
        parts[r][...] = acc[lead:lead + span]


def rest_kernel(
    counts, rows, voxels, far_slots, far_rows, far_counts, sino, tiles, *rest,
    role, gates, bins, slots, send, starts, gots, local_rows
):
    first, got, rest = rest[:starts], rest[starts:starts + gots], rest[starts + gots:]
    which = list_of(role)
    count = counts[which]
    per = slots // CHUNKS
    lead = bins // 2 * gates
    span = VT * gates

    if role < SPLIT:
        *out, acc = rest
        buf = tiles.at[role]
    else:
        *out, acc, buf, sems = rest

    def chunk_copy(c):
        return pltpu.make_async_copy(
            tiles.at[which, pl.ds(c * per, per)], buf.at[pl.ds(c * per, per)], sems.at[c]
        )

    for c in range(CHUNKS if role >= SPLIT else 0):
        @pl.when(c * per < count)
        def _():
            chunk_copy(c).start()

    acc[0:lead] = jnp.zeros((lead, acc.shape[1]), jnp.float32)
    acc[lead + span:] = jnp.zeros((acc.shape[0] - lead - span, acc.shape[1]), jnp.float32)
    if starts:
        acc[lead:lead + span] = first[0][...]
    else:
        acc[lead:lead + span] = jnp.zeros((span, acc.shape[1]), jnp.float32)
    for i, piece in enumerate(got):
        size = span // gots
        acc[lead + i * size:lead + (i + 1) * size] += widen(piece)
    for c in range(CHUNKS if role >= SPLIT else 0):
        @pl.when(c * per < count)
        def _():
            chunk_copy(c).wait()
            add_slots(
                acc, buf, sino, lambda k: k, lambda k, j: place_of(rows[which, j], local_rows),
                lambda j: voxels[which, j], c * per, jnp.minimum(count, (c + 1) * per), gates, bins,
            )
    if role < SPLIT:
        add_slots(
            acc, buf, sino, lambda k: far_slots[role, k], lambda k, j: far_rows[role, k],
            lambda j: voxels[which, j], 0, far_counts[role], gates, bins,
        )
    if not send:
        out[0][...] = acc[lead:lead + span]
    else:
        for i, piece in enumerate(out):
            size = span // len(out)
            encode(acc[lead + i * size:lead + (i + 1) * size], piece)


def encode(image, out):
    span, width = image.shape
    values = image.reshape(span // GROUP, GROUP, width)
    top = jnp.maximum(jnp.max(jnp.abs(values), axis=1), 1e-30)
    code = jnp.ceil(STEPS * jnp.log2(top))
    inv = TOP * jnp.exp2(code * (-1.0 / STEPS))
    q = jnp.clip(jnp.round(values * inv[:, None, :]), -TOP, TOP)
    out[0:span] = q.astype(jnp.int32).astype(jnp.int16).reshape(span, width)
    out[span:] = code.astype(jnp.int32).astype(jnp.int16)


def widen(sent):
    span, width = sent.shape[0] * GROUP // (GROUP + 1), sent.shape[1]
    code = sent[span:].astype(jnp.int32).astype(jnp.float32)
    scale = jnp.exp2(code * (1.0 / STEPS)) * (1.0 / TOP)
    values = sent[0:span].astype(jnp.int32).astype(jnp.float32)
    values = values.reshape(span // GROUP, GROUP, width) * scale[:, None, :]
    return values.reshape(span, width)


def join_image(own, far, near, *rest):
    *pair, out = rest
    size = own.shape[0] // len(pair)
    out[...] = own[...] + widen(far) + widen(near)
    for i, piece in enumerate(pair):
        out[i * size:(i + 1) * size] += widen(piece)


def local(residual, tile_values, row_index, voxel_index, slot_count, tof_shift):
    local_rows, gates, bins, depth = residual.shape[1:]
    lists, slots, _, width = tile_values.shape[2:]
    size = gates * bins
    span = VT * gates
    tiles = tile_values[0, 0]
    rows = row_index[0, 0]
    voxels = voxel_index[0, 0]
    counts = slot_count[0, 0]
    slabs = lax.axis_size("slab")
    blocks = lax.axis_size("blk")
    res = residual[0].reshape(local_rows, size, depth)
    others = [
        lax.ppermute(res, "blk", [(i, (i + hop) % blocks) for i in range(blocks)])
        for hop in range(1, blocks)
    ]
    params = pltpu.CompilerParams(vmem_limit_bytes=LIMIT)

    acc = pltpu.VMEM((span + bins * gates + size, width), jnp.float32)
    image = jax.ShapeDtypeStruct((span, width), jnp.float32)
    table = jax.ShapeDtypeStruct((SPLIT, slots), jnp.int32)
    *parts, mine, held_tiles, far_slots, far_rows, far_counts = pl.pallas_call(
        partial(first_kernel, gates=gates, bins=bins, slots=slots),
        out_shape=[image] * SPLIT
        + [jax.ShapeDtypeStruct(res.shape, res.dtype)]
        + [jax.ShapeDtypeStruct((SPLIT, slots, depth, width), tiles.dtype)]
        + [table, table, jax.ShapeDtypeStruct((SPLIT,), jnp.int32)],
        in_specs=[SMEM] * 4 + [HBM, HBM],
        out_specs=[VMEM] * (SPLIT + 2) + [SMEM] * 3,
        scratch_shapes=[
            pltpu.VMEM(res.shape, res.dtype),
            acc,
            pltpu.SMEM((slots,), jnp.int32),
            pltpu.SemaphoreType.DMA(()),
            pltpu.SemaphoreType.DMA((SPLIT, CHUNKS)),
        ],
        compiler_params=params,
        cost_estimate=COST,
    )(tof_shift, counts, rows, voxels, res, tiles)

    sino = pl.pallas_call(
        partial(join_kernel, gates=gates, bins=bins),
        out_shape=jax.ShapeDtypeStruct((local_rows * blocks, size, depth), jnp.bfloat16),
        in_specs=[SMEM, VMEM, VMEM],
        out_specs=VMEM,
        compiler_params=params,
        cost_estimate=COST,
    )(tof_shift, mine, others[0] if len(others) == 1 else jnp.concatenate(others))

    def run(role, after, got=()):
        held = counts
        if after is not None:
            held, after = lax.optimization_barrier((counts, after))
        starts = [parts[role]] if role < SPLIT else []
        pieces = {OWN: 0, IN1: PIECES, IN2: PIECES}.get(role, 1)
        rows_out = span // max(pieces, 1)
        shape = jax.ShapeDtypeStruct((rows_out + rows_out // GROUP, width), jnp.int16)
        out = pl.pallas_call(
            partial(
                rest_kernel, role=role, gates=gates, bins=bins, slots=slots, send=pieces > 0,
                starts=len(starts), gots=len(got), local_rows=local_rows,
            ),
            out_shape=[shape] * pieces if pieces else [image],
            in_specs=[SMEM] * 6 + [VMEM, VMEM if role < SPLIT else HBM] + [VMEM] * (len(starts) + len(got)),
            out_specs=[VMEM] * max(pieces, 1),
            scratch_shapes=[acc]
            if role < SPLIT
            else [
                acc,
                pltpu.VMEM((slots, depth, width), jnp.bfloat16),
                pltpu.SemaphoreType.DMA((CHUNKS,)),
            ],
            compiler_params=params,
            cost_estimate=COST,
        )(held, rows, voxels, far_slots, far_rows, far_counts, sino,
          held_tiles if role < SPLIT else tiles, *starts, *got)
        return out, after

    def pass_on(sent, route):
        return [lax.ppermute(piece, "slab", route) for piece in sent]

    mate = [(i, i ^ 1) for i in range(slabs)]

    def outward(distance):
        route = []
        for i in range(slabs):
            j = i + (distance if i % 2 else -distance)
            if 0 <= j < slabs:
                route.append((i, j))
        return route

    in2, _ = run(IN2, None)
    far, in2 = run(FAR, in2)
    near, far = run(NEAR, far, pass_on(in2, mate))
    far = pass_on(far, outward(2))
    in1, near = run(IN1, near)
    near = pass_on(near, outward(1))
    own, in1 = run(OWN, in1)
    in1 = pass_on(in1, mate)
    image_sum = pl.pallas_call(
        join_image,
        out_shape=image,
        in_specs=[VMEM] * (3 + PIECES),
        out_specs=VMEM,
        compiler_params=params,
        cost_estimate=COST,
    )(*own, *far, *near, *in1)
    return image_sum.reshape(1, VT, gates, width)


def solution(mesh):
    placed = (
        P("slab", "blk", None, None, None),
        P("slab", "blk", None, None, None, None),
        P("slab", "blk", None, None),
        P("slab", "blk", None, None),
        P("slab", "blk", None),
        P(),
    )
    return jax.shard_map(
        local, mesh=mesh, in_specs=placed, out_specs=P("slab", "blk", None, None), check_vma=False
    )
```

```python
from functools import partial

import jax
import jax.numpy as jnp
from jax import lax
from jax.experimental import pallas as pl
from jax.experimental.pallas import tpu as pltpu
from jax.sharding import PartitionSpec as P

VT = 256
UNROLL = 4
CHUNKS = 4
GROUP = 64
TOP = 32767.0
STEPS = 8.0
LIMIT = 43 * 1024 * 1024
SMEM = pl.BlockSpec(memory_space=pltpu.SMEM)
VMEM = pl.BlockSpec(memory_space=pltpu.VMEM)
HBM = pl.BlockSpec(memory_space=pltpu.HBM)

FAR, IN2, NEAR, IN1, OWN = range(5)
REACH = (2, -2, 1, -1, 0)
PIECES = 2
SPLIT = 3
COST = pl.CostEstimate(flops=1000, bytes_accessed=1000, transcendentals=0)


def add_slots(acc, buf, sino, slot_of, row_of, voxel_of, begin, total, gates, bins):
    size = gates * bins
    dump = VT + bins

    def group(i, carry):
        first = begin + i * UNROLL
        for u in range(UNROLL):
            k = first + u
            live = k < total
            j = jnp.where(live, slot_of(k), 0)
            row = jnp.where(live, row_of(k, j), 0)
            v = jnp.where(live, voxel_of(j), dump)
            at = pl.ds(pl.multiple_of(v * gates, gates), size)
            acc[at] += jnp.dot(sino[row], buf[j], preferred_element_type=jnp.float32)
        return carry

    lax.fori_loop(0, (total - begin + UNROLL - 1) // UNROLL, group, 0)


def list_of(role):
    sign = 2 * lax.rem(lax.axis_index("slab"), 2) - 1
    return REACH[0] + REACH[role] * sign


def place_of(row, local_rows):
    block, blocks = lax.axis_index("blk"), lax.axis_size("blk")
    hop = block - lax.div(row, local_rows)
    hop = jnp.where(hop < 0, hop + blocks, hop)
    return hop * local_rows + lax.rem(row, local_rows)


def sorter(shift, gates, bins):
    size = gates * bins
    src = lax.broadcasted_iota(jnp.int32, (1, size), 1)
    bin_of = lax.rem(src, bins)
    place = jnp.zeros((1, size), jnp.int32)
    for t in range(bins):
        place = jnp.where(bin_of == t, shift[t] + bins // 2, place)
    target = place * gates + lax.div(src, bins)
    dst = lax.broadcasted_iota(jnp.int32, (size, size), 0)
    return (target == dst).astype(jnp.float32).astype(jnp.bfloat16)


def reorder(mat, tile):
    return jnp.dot(mat, tile, preferred_element_type=jnp.float32).astype(jnp.bfloat16)


def join_kernel(shift, mine, others, out, *, gates, bins):
    mat = sorter(shift, gates, bins)
    local_rows = mine.shape[0]
    out[0:local_rows] = mine[...]

    def one(i, carry):
        out[local_rows + i] = reorder(mat, others[i])
        return carry

    lax.fori_loop(0, others.shape[0], one, 0, unroll=4)


def first_kernel(
    shift, counts, rows, voxels, res, tiles, *rest, gates, bins, slots
):
    *parts, sino, buf, far_slots, far_rows, far_counts, raw, acc, near_slots, raw_sem, sems = rest
    local_rows = res.shape[0]
    per = slots // CHUNKS
    lead = bins // 2 * gates
    span = VT * gates

    load = pltpu.make_async_copy(res, raw, raw_sem)
    load.start()

    def chunk_copy(r, c):
        return pltpu.make_async_copy(
            tiles.at[list_of(r), pl.ds(c * per, per)], buf.at[r, pl.ds(c * per, per)], sems.at[r, c]
        )

    for r in range(SPLIT):
        for c in range(CHUNKS):
            @pl.when(c * per < counts[list_of(r)])
            def _():
                chunk_copy(r, c).start()

    mat = sorter(shift, gates, bins)
    load.wait()
    for i in range(local_rows):
        sino[i] = reorder(mat, raw[i])

    for r in range(SPLIT):
        which = list_of(r)
        count = counts[which]

        def split(j, found):
            here, there = found
            row = place_of(rows[which, j], local_rows)
            near_slots[here] = j
            far_slots[r, there] = j
            far_rows[r, there] = row
            step = (row < local_rows).astype(jnp.int32)
            return here + step, there + 1 - step

        here, there = lax.fori_loop(0, count, split, (0, 0))
        far_counts[r] = there
        acc[...] = jnp.zeros(acc.shape, jnp.float32)
        for c in range(CHUNKS):
            @pl.when(c * per < count)
            def _():
                chunk_copy(r, c).wait()
        add_slots(
            acc, buf.at[r], sino, lambda k: near_slots[k],
            lambda k, j: lax.rem(rows[which, j], local_rows), lambda j: voxels[which, j],
            0, here, gates, bins,
        )
        parts[r][...] = acc[lead:lead + span]


def rest_kernel(
    counts, rows, voxels, far_slots, far_rows, far_counts, sino, tiles, *rest,
    role, gates, bins, slots, send, starts, gots, local_rows
):
    first, got, rest = rest[:starts], rest[starts:starts + gots], rest[starts + gots:]
    which = list_of(role)
    count = counts[which]
    per = slots // CHUNKS
    lead = bins // 2 * gates
    span = VT * gates

    if role < SPLIT:
        *out, acc = rest
        buf = tiles.at[role]
    else:
        *out, acc, buf, sems = rest

    def chunk_copy(c):
        return pltpu.make_async_copy(
            tiles.at[which, pl.ds(c * per, per)], buf.at[pl.ds(c * per, per)], sems.at[c]
        )

    for c in range(CHUNKS if role >= SPLIT else 0):
        @pl.when(c * per < count)
        def _():
            chunk_copy(c).start()

    acc[0:lead] = jnp.zeros((lead, acc.shape[1]), jnp.float32)
    acc[lead + span:] = jnp.zeros((acc.shape[0] - lead - span, acc.shape[1]), jnp.float32)
    if starts:
        acc[lead:lead + span] = first[0][...]
    else:
        acc[lead:lead + span] = jnp.zeros((span, acc.shape[1]), jnp.float32)
    for i, piece in enumerate(got):
        size = span // gots
        acc[lead + i * size:lead + (i + 1) * size] += widen(piece)
    for c in range(CHUNKS if role >= SPLIT else 0):
        @pl.when(c * per < count)
        def _():
            chunk_copy(c).wait()
            add_slots(
                acc, buf, sino, lambda k: k, lambda k, j: place_of(rows[which, j], local_rows),
                lambda j: voxels[which, j], c * per, jnp.minimum(count, (c + 1) * per), gates, bins,
            )
    if role < SPLIT:
        add_slots(
            acc, buf, sino, lambda k: far_slots[role, k], lambda k, j: far_rows[role, k],
            lambda j: voxels[which, j], 0, far_counts[role], gates, bins,
        )
    if not send:
        out[0][...] = acc[lead:lead + span]
    else:
        for i, piece in enumerate(out):
            size = span // len(out)
            encode(acc[lead + i * size:lead + (i + 1) * size], piece)


def encode(image, out):
    span, width = image.shape
    values = image.reshape(span // GROUP, GROUP, width)
    top = jnp.maximum(jnp.max(jnp.abs(values), axis=1), 1e-30)
    code = jnp.ceil(STEPS * jnp.log2(top))
    inv = TOP * jnp.exp2(code * (-1.0 / STEPS))
    q = jnp.clip(jnp.round(values * inv[:, None, :]), -TOP, TOP)
    out[0:span] = q.astype(jnp.int32).astype(jnp.int16).reshape(span, width)
    out[span:] = code.astype(jnp.int32).astype(jnp.int16)


def widen(sent):
    span, width = sent.shape[0] * GROUP // (GROUP + 1), sent.shape[1]
    code = sent[span:].astype(jnp.int32).astype(jnp.float32)
    scale = jnp.exp2(code * (1.0 / STEPS)) * (1.0 / TOP)
    values = sent[0:span].astype(jnp.int32).astype(jnp.float32)
    values = values.reshape(span // GROUP, GROUP, width) * scale[:, None, :]
    return values.reshape(span, width)


def join_image(own, far, near, *rest):
    *pair, out = rest
    size = own.shape[0] // len(pair)
    out[...] = own[...] + widen(far) + widen(near)
    for i, piece in enumerate(pair):
        out[i * size:(i + 1) * size] += widen(piece)


def local(residual, tile_values, row_index, voxel_index, slot_count, tof_shift):
    local_rows, gates, bins, depth = residual.shape[1:]
    lists, slots, _, width = tile_values.shape[2:]
    size = gates * bins
    span = VT * gates
    tiles = tile_values[0, 0]
    rows = row_index[0, 0]
    voxels = voxel_index[0, 0]
    counts = slot_count[0, 0]
    slabs = lax.axis_size("slab")
    blocks = lax.axis_size("blk")
    res = residual[0].reshape(local_rows, size, depth)
    others = [
        lax.ppermute(res, "blk", [(i, (i + hop) % blocks) for i in range(blocks)])
        for hop in range(1, blocks)
    ]
    params = pltpu.CompilerParams(vmem_limit_bytes=LIMIT)

    acc = pltpu.VMEM((span + bins * gates + size, width), jnp.float32)
    image = jax.ShapeDtypeStruct((span, width), jnp.float32)
    table = jax.ShapeDtypeStruct((SPLIT, slots), jnp.int32)
    *parts, mine, held_tiles, far_slots, far_rows, far_counts = pl.pallas_call(
        partial(first_kernel, gates=gates, bins=bins, slots=slots),
        out_shape=[image] * SPLIT
        + [jax.ShapeDtypeStruct(res.shape, res.dtype)]
        + [jax.ShapeDtypeStruct((SPLIT, slots, depth, width), tiles.dtype)]
        + [table, table, jax.ShapeDtypeStruct((SPLIT,), jnp.int32)],
        in_specs=[SMEM] * 4 + [HBM, HBM],
        out_specs=[VMEM] * (SPLIT + 2) + [SMEM] * 3,
        scratch_shapes=[
            pltpu.VMEM(res.shape, res.dtype),
            acc,
            pltpu.SMEM((slots,), jnp.int32),
            pltpu.SemaphoreType.DMA(()),
            pltpu.SemaphoreType.DMA((SPLIT, CHUNKS)),
        ],
        compiler_params=params,
        cost_estimate=COST,
    )(tof_shift, counts, rows, voxels, res, tiles)

    sino = pl.pallas_call(
        partial(join_kernel, gates=gates, bins=bins),
        out_shape=jax.ShapeDtypeStruct((local_rows * blocks, size, depth), jnp.bfloat16),
        in_specs=[SMEM, VMEM, VMEM],
        out_specs=VMEM,
        compiler_params=params,
        cost_estimate=COST,
    )(tof_shift, mine, others[0] if len(others) == 1 else jnp.concatenate(others))

    def run(role, after, got=()):
        held = counts
        if after is not None:
            held, after = lax.optimization_barrier((counts, after))
        starts = [parts[role]] if role < SPLIT else []
        pieces = {OWN: 0, IN1: PIECES, IN2: PIECES}.get(role, 1)
        rows_out = span // max(pieces, 1)
        shape = jax.ShapeDtypeStruct((rows_out + rows_out // GROUP, width), jnp.int16)
        out = pl.pallas_call(
            partial(
                rest_kernel, role=role, gates=gates, bins=bins, slots=slots, send=pieces > 0,
                starts=len(starts), gots=len(got), local_rows=local_rows,
            ),
            out_shape=[shape] * pieces if pieces else [image],
            in_specs=[SMEM] * 6 + [VMEM, VMEM if role < SPLIT else HBM] + [VMEM] * (len(starts) + len(got)),
            out_specs=[VMEM] * max(pieces, 1),
            scratch_shapes=[acc]
            if role < SPLIT
            else [
                acc,
                pltpu.VMEM((slots, depth, width), jnp.bfloat16),
                pltpu.SemaphoreType.DMA((CHUNKS,)),
            ],
            compiler_params=params,
            cost_estimate=COST,
        )(held, rows, voxels, far_slots, far_rows, far_counts, sino,
          held_tiles if role < SPLIT else tiles, *starts, *got)
        return out, after

    def pass_on(sent, route):
        return [lax.ppermute(piece, "slab", route) for piece in sent]

    mate = [(i, i ^ 1) for i in range(slabs)]

    def outward(distance):
        route = []
        for i in range(slabs):
            j = i + (distance if i % 2 else -distance)
            if 0 <= j < slabs:
                route.append((i, j))
        return route

    in2, _ = run(IN2, None)
    far, in2 = run(FAR, in2)
    near, far = run(NEAR, far, pass_on(in2, mate))
    far = pass_on(far, outward(2))
    in1, near = run(IN1, near)
    near = pass_on(near, outward(1))
    own, in1 = run(OWN, in1)
    in1 = pass_on(in1, mate)
    image_sum = pl.pallas_call(
        join_image,
        out_shape=image,
        in_specs=[VMEM] * (3 + PIECES),
        out_specs=VMEM,
        compiler_params=params,
        cost_estimate=COST,
    )(*own, *far, *near, *in1)
    return image_sum.reshape(1, VT, gates, width)


def solution(mesh):
    placed = (
        P("slab", "blk", None, None, None),
        P("slab", "blk", None, None, None, None),
        P("slab", "blk", None, None),
        P("slab", "blk", None, None),
        P("slab", "blk", None),
        P(),
    )
    return jax.shard_map(
        local, mesh=mesh, in_specs=placed, out_specs=P("slab", "blk", None, None), check_vma=False
    )
```
